32 devices in a mesh: section: 1, ctx: 32 (over z, y, x, core).
Axes of the slice: x: 2, y: 2, z: 4, core: 2. Of those that a mesh axis runs over, the one named last changes fastest.
Arguments:
- hidden: bfloat16 [4096, 8192], P(('section', 'ctx')), may hold values from -12 to 12
- norm_gain: bfloat16 [8192], replicated, may hold values from 0.25 to 1.75
- w_qkv: bfloat16 [8192, 768], P('ctx'), may hold values from -2 to 2
- doc_ids: int32 [4096], P(('section', 'ctx')), may hold values from 0 to 31, never falling along the last dimension, each value on 1 to 1024 neighbouring positions
- target: int32 [4096], P(('section', 'ctx')), may hold values from 0 to 31, as said below
Outputs:
- attended: bfloat16 [4096, 512], P(('section', 'ctx'))
The draws below stay inside these ranges and needn't reach their ends.
Inputs may be any that keep to these rules, and one draw needn't show every extreme that they name: Each device is the target of exactly 128 tokens; the tokens of one device with one target number 0, 4 or 8, and 8 occurs in every draw.
All inputs are finite; a program needn't handle non-finite values.
Results may differ from the reference program's by a relative error of at most 0.0078.
Values may be sent and summed in bfloat16 or wider, within the bound.
A program may use at most 64 MiB of HBM per device.

```python
import math
import jax
import jax.numpy as jnp
import numpy as np
from jax import lax

D = 8192
HD = 128
QH = 4
TOK_DEV = 128
TOKENS = 4096
QKVW = 768
DOCS = 32
MOST = 1024
N_CTX = 32


score_level = 260.0


def pattern_row(width):
    index = jnp.arange(width, dtype=jnp.int32)
    level = (index * 29 + index // 5 * 13) % 9 - 4
    return level.astype(jnp.float32) * (1.0 / math.sqrt(20.0 / 3.0))


def draw_hidden(key, part):
    key = jax.random.fold_in(key, 11)
    noise_key, pick_key, level_key = jax.random.split(key, 3)
    noise = jnp.clip(jax.random.normal(noise_key, (TOKENS, D), jnp.float32), -4.0, 4.0)
    share = 1.0 / 16.0
    lowest = 1.0
    highest = 4.0
    picked = jax.random.bernoulli(pick_key, share, (TOKENS,))
    strength = jax.random.uniform(level_key, (TOKENS,), jnp.float32, lowest, highest)
    amount = jnp.where(picked, strength, 0.0)
    return (noise + amount[:, None] * pattern_row(D)[None, :]).astype(jnp.bfloat16)


def draw_w_qkv(key, part):
    key = jax.random.fold_in(key, 13)
    noise_key, sign_key, head_key = jax.random.split(key, 3)
    scale = 1.0 / math.sqrt(D)
    noise = jnp.clip(jax.random.normal(noise_key, (D, QKVW), jnp.float32), -6.0, 6.0) * scale
    half = HD // 2
    low = half - 3 * half // 8
    planted = 2 * (half - low)
    alpha = math.sqrt(score_level * math.sqrt(HD) / (D * planted))
    column = jnp.arange(HD, dtype=jnp.int32)
    inside = (column % half >= low).astype(jnp.float32)
    signs = jnp.where(jax.random.bernoulli(sign_key, 0.5, (HD,)), 1.0, -1.0) * inside
    gammas = jax.random.uniform(head_key, (QH,), jnp.float32, 0.8, 1.2)
    query_part = (gammas[:, None] * signs[None, :]).reshape(QH * HD)
    planted_row = jnp.concatenate([query_part, signs, jnp.zeros((HD,), jnp.float32)]) * alpha
    direction = pattern_row(D) * scale
    return (noise + direction[:, None] * planted_row[None, :]).astype(jnp.bfloat16)


def draw_target(key, part):
    key = jax.random.fold_in(key, 7)
    base = TOK_DEV // N_CTX
    shift_val = jax.random.randint(jax.random.fold_in(key, 1), (), 0, N_CTX)
    source = jnp.arange(N_CTX, dtype=jnp.int32)[:, None]
    destin = jnp.arange(N_CTX, dtype=jnp.int32)[None, :]
    offset = (destin - source - shift_val) % N_CTX
    counts = base + base * (offset == 0).astype(jnp.int32) - base * (offset == 1).astype(jnp.int32)
    cumul = jnp.cumsum(counts, axis=1)
    slots = jnp.arange(TOK_DEV, dtype=jnp.int32)
    dest_list = jnp.sum((cumul[:, None, :] <= slots[None, :, None]).astype(jnp.int32), axis=2)
    keys_all = jax.random.split(jax.random.fold_in(key, 2), N_CTX)
    perms = jax.vmap(lambda sub_key: jax.random.permutation(sub_key, TOK_DEV))(keys_all)
    dest_list = jnp.take_along_axis(dest_list, perms, axis=1)
    return dest_list.reshape(-1).astype(jnp.int32)


def length_profile(count, total, most, lean):
    loads = [(1 << 20) // math.isqrt(standing ** lean) + 1 for standing in range(2, count + 1)]
    spare, given = total - most - (count - 1), [1] * (count - 1)
    while spare > 0:
        candidates = [i for i in range(count - 1) if given[i] < most]
        pool, left = sum([loads[i] for i in candidates]), spare
        for i in candidates:
            more = min(most - given[i], max(1, left * loads[i] // pool), spare)
            given[i] = given[i] + more
            spare = spare - more
    return np.array([most] + given)


def uneven_parts(own_key, count, total, reach, skew):
    if count == 2:
        one = jax.random.randint(own_key, (), max(1, total - reach), min(reach, total - 1) + 1)
        return jnp.stack([one, total - one])
    sizes = jnp.asarray(length_profile(count, total, reach, skew), jnp.int32)
    twos = (count - 1) // 2
    donor, receiver = sizes[1:1 + 2 * twos:2], sizes[2:2 + 2 * twos:2]
    room = jnp.minimum(donor - 1, reach - receiver)
    passed = jax.random.randint(jax.random.fold_in(own_key, 1), (twos,), 0, 1 << 20) % (room + 1)
    sizes = sizes.at[1:1 + 2 * twos:2].set(donor - passed).at[2:2 + 2 * twos:2].set(receiver + passed)
    return sizes[jax.random.permutation(jax.random.fold_in(own_key, 2), count)]


def setup_inputs(seed: int = 0, part: int = 0) -> dict:
    key_list = jax.random.split(jax.random.key(seed), 6)
    part_splits = jax.random.split(jax.random.fold_in(key_list[5], part), 6)
    return {
        "hidden": draw_hidden(jax.random.fold_in(jax.random.fold_in(key_list[5], part), 71), part),
        "norm_gain": jnp.clip(1.0 + 0.15 * jax.random.normal(key_list[1], (D,), jnp.float32), 0.25, 1.75).astype(jnp.bfloat16),
        "w_qkv": draw_w_qkv(jax.random.fold_in(key_list[5], 71), part),
        "doc_ids": jnp.searchsorted(jnp.cumsum(uneven_parts(part_splits[3], DOCS, TOKENS, MOST, 1)), jnp.arange(TOKENS), side="right").astype(jnp.int32),
        "target": draw_target(jax.random.fold_in(jax.random.fold_in(key_list[5], part), 71), part),
    }


def rotate(block, position):
    half = block.shape[-1] // 2
    freqs = 500000.0 ** (-(jnp.arange(half, dtype=jnp.float32) * 2.0) / block.shape[-1])
    angle = position.astype(jnp.float32)[:, None, None] * freqs[None, None, :]
    cosine = jnp.cos(angle)
    sine = jnp.sin(angle)
    first = block[..., :half]
    second = block[..., half:]
    return jnp.concatenate([first * cosine - second * sine, second * cosine + first * sine], axis=-1)

def reference(hidden, norm_gain, w_qkv, doc_ids, target):
    values_x = hidden.astype(jnp.float32)
    scale_norm = lax.rsqrt(lax.optimization_barrier(jnp.mean(values_x * values_x, axis=1, keepdims=True)) + 1e-05)
    normed = (values_x * scale_norm * norm_gain.astype(jnp.float32)).astype(jnp.bfloat16)
    proj = jnp.dot(normed, w_qkv, preferred_element_type=jnp.float32)
    index = jnp.arange(TOKENS, dtype=jnp.int32)
    first_index = jnp.searchsorted(doc_ids, doc_ids, side='left').astype(jnp.int32)
    position = index - first_index
    query = rotate(proj[:, :QH * HD].reshape(TOKENS, QH, HD), position).astype(jnp.bfloat16)
    key_rot = rotate(proj[:, QH * HD:(QH + 1) * HD].reshape(TOKENS, 1, HD), position)[:, 0, :].astype(jnp.bfloat16)
    value = proj[:, (QH + 1) * HD:].astype(jnp.bfloat16)
    block_len = math.gcd(TOKENS, 512)
    key_f = key_rot.astype(jnp.float32)
    value_f = value.astype(jnp.float32)

    def one_block(block_id):
        lo = block_id * block_len
        query_b = lax.dynamic_slice_in_dim(query, lo, block_len, 0).astype(jnp.float32)
        doc_b = lax.dynamic_slice_in_dim(doc_ids, lo, block_len, 0)
        idx_b = lax.dynamic_slice_in_dim(index, lo, block_len, 0)
        scores = jnp.einsum('qhd,kd->qhk', query_b, key_f) / math.sqrt(HD)
        visible = (doc_ids[None, :] == doc_b[:, None]) & (index[None, :] <= idx_b[:, None])
        visible = visible[:, None, :]
        largest = lax.optimization_barrier(jnp.max(jnp.where(visible, scores, -1e+30), axis=2, keepdims=True))
        weights = jnp.where(visible, jnp.exp(scores - largest), 0.0)
        total = lax.optimization_barrier(jnp.sum(weights, axis=2))
        rounded = weights.astype(jnp.bfloat16).astype(jnp.float32)
        summed = jnp.einsum('qhk,kd->qhd', rounded, value_f)
        return (summed / total[:, :, None]).reshape(block_len, QH * HD)
    blocks = lax.map(one_block, jnp.arange(TOKENS // block_len, dtype=jnp.int32))
    out = blocks.reshape(TOKENS, QH * HD)
    order = jnp.argsort(target, stable=True).astype(jnp.int32)
    return out[order].astype(jnp.bfloat16)
```

```python
import functools
import math

import jax
import jax.numpy as jnp
from jax import lax
from jax.experimental import pallas as pl
from jax.experimental.pallas import tpu as pltpu
from jax.sharding import PartitionSpec as P

HD = 128
QH = 4
MOST = 1024
NCH = 3
CW = 256
COLS = (2, 0, 1)
PLACE = (0, 2, 1, 3)
MESH = pl.DeviceIdType.MESH


def rotate(block, cosine, sine):
    return block * cosine + pltpu.roll(block, HD // 2, 1) * sine


def kernel(
    n_dev, hidden_ref, gain_ref, w_ref, doc_row_ref, doc_col_ref, tgt_row_ref, freq_ref, packed_ref,
    nsend, xg, wbuf, part, crecv, xsend, xrecv, kvbuf, dwin, bias, outbuf,
    h_send, h_recv, h_own, z_send, z_recv, y_send, y_recv, c_send, c_recv, x_send, x_recv,
    kv_send, kv_recv, d_send, d_recv,
):
    rows = hidden_ref.shape[0]
    depth = w_ref.shape[0]
    width = hidden_ref.shape[1]
    back = kvbuf.shape[0] - 1
    nz = n_dev // 8
    shards = n_dev // 4
    me = lax.axis_index("ctx")
    z, y, x, c = me // 8, (me // 4) % 2, (me // 2) % 2, me % 2
    spot = 2 * c + x
    shard = me // 4

    def remote(src, dst, send, recv, dev):
        return pltpu.make_async_remote_copy(
            src_ref=src, dst_ref=dst, send_sem=send, recv_sem=recv,
            device_id={"ctx": dev}, device_id_type=MESH,
        )

    dwin[...] = jnp.full_like(dwin, -1)
    kvbuf[...] = jnp.zeros_like(kvbuf)
    for n in range(NCH):
        wbuf[n, pl.ds(pl.multiple_of(shard * depth, depth), depth), :] = w_ref[
            :, COLS[n] * CW : (COLS[n] + 1) * CW
        ]
    dwin[back] = doc_row_ref[...]

    barrier = pltpu.get_barrier_semaphore()

    def greet(d, carry):
        pl.semaphore_signal(
            barrier, inc=1, device_id={"ctx": lax.rem(me + d, n_dev)}, device_id_type=MESH
        )
        return carry

    lax.fori_loop(1, n_dev, greet, 0)
    pl.semaphore_wait(barrier, n_dev - 1)

    y_dev = z * 8 + (1 - y) * 4 + x * 2 + c
    c_dev = z * 8 + y * 4 + x * 2 + (1 - c)
    x_dev = z * 8 + y * 4 + (1 - x) * 2 + c

    def slot(n, j):
        return wbuf.at[n, pl.ds(pl.multiple_of(j * depth, depth), depth), :]

    def y_copy(n, dz):
        j = lax.rem(z - dz + nz, nz) * 2 + y
        return remote(slot(n, j), slot(n, j), y_send.at[n, dz], y_recv.at[n, dz], y_dev)

    def z_copy(n, dz):
        dev = lax.rem(z + dz, nz) * 8 + y * 4 + x * 2 + c
        return remote(slot(n, shard), slot(n, shard), z_send.at[n, dz], z_recv.at[n, dz], dev)

    def d_copy(d):
        return remote(
            dwin.at[back], dwin.at[back - d], d_send.at[d - 1], d_recv.at[d - 1],
            lax.rem(me + d, n_dev),
        )

    def kv_copy(d):
        return remote(
            kvbuf.at[back], kvbuf.at[back - d], kv_send.at[d - 1], kv_recv.at[d - 1],
            lax.rem(me + d, n_dev),
        )

    def each_later(do):
        for d in range(1, back + 1):
            pl.when(me + d < n_dev)(functools.partial(do, d))

    def each_earlier(do):
        for d in range(1, back + 1):
            pl.when(me >= d)(functools.partial(do, d))

    each_later(lambda d: d_copy(d).start())
    for n in range(NCH):
        for dz in range(nz):
            if dz:
                z_copy(n, dz).start()
            else:
                y_copy(n, 0).start()

    step = 16

    def norm_rows(i, carry):
        at = pl.ds(pl.multiple_of(i * step, step), step)
        total = jnp.zeros((step, CW), jnp.float32)
        for b in range(width // CW):
            v = hidden_ref[at, b * CW : (b + 1) * CW].astype(jnp.float32)
            total = total + v * v
        scale = lax.rsqrt(jnp.sum(total, axis=1, keepdims=True) * (1.0 / width) + 1e-05)
        for b in range(width // depth):
            v = hidden_ref[at, b * depth : (b + 1) * depth].astype(jnp.float32)
            g = gain_ref[:, b * depth : (b + 1) * depth]
            nsend[PLACE[b % 4], at, (b // 4) * depth : (b // 4 + 1) * depth] = (
                v * scale * g
            ).astype(jnp.bfloat16)
        return carry

    lax.fori_loop(0, rows // step, norm_rows, 0)

    def h_copy(k):
        dx, dc = ((1, 0), (1, 1), (0, 1))[k]
        ox = 1 - x if dx else x
        oc = 1 - c if dc else c
        return remote(
            nsend.at[2 * oc + ox], xg.at[spot], h_send.at[k], h_recv.at[k],
            z * 8 + y * 4 + ox * 2 + oc,
        )

    for k in range(3):
        h_copy(k).start()
    own = pltpu.make_async_copy(nsend.at[spot], xg.at[spot], h_own)
    own.start()

    def forward(n):
        for dz in range(1, nz):
            z_copy(n, dz).wait_recv()
            y_copy(n, dz).start()

    each_earlier(lambda d: d_copy(d).wait_recv())
    count = jnp.zeros((rows, 1), jnp.float32)
    for s in range(back + 1):
        seen = doc_col_ref[...] == dwin[s, 0:1, :]
        if s == back:
            seen = seen & (
                lax.broadcasted_iota(jnp.int32, (rows, rows), 1)
                <= lax.broadcasted_iota(jnp.int32, (rows, rows), 0)
            )
        bias[:, s * rows : (s + 1) * rows] = jnp.where(seen, 0.0, -1e30)
        count = count + jnp.sum(jnp.where(seen, 1.0, 0.0), axis=1, keepdims=True)
    angle = (count - 1.0) * freq_ref[...]
    cosine = jnp.cos(angle)
    sine = jnp.sin(angle) * jnp.where(
        lax.broadcasted_iota(jnp.int32, (rows, HD), 1) < HD // 2, -1.0, 1.0
    )

    def matmul(n):
        for dz in range(nz):
            y_copy(n, dz).wait_recv()
        left = xg[...].reshape(4 * rows, xg.shape[2])
        part[n] = jnp.dot(left, wbuf[n], preferred_element_type=jnp.float32).reshape(
            2, 2, rows, CW
        )

    def c_copy(n):
        return remote(part.at[n, 1 - c], crecv.at[n], c_send.at[n], c_recv.at[n], c_dev)

    def x_copy(n):
        return remote(xsend.at[n], xrecv.at[n], x_send.at[n], x_recv.at[n], x_dev)

    def cross(n):
        c_copy(n).wait_recv()
        xsend[n] = part[n, c, 1 - x] + crecv[n, 1 - x]
        x_copy(n).start()

    def finish(n):
        x_copy(n).wait_recv()
        return part[n, c, x] + crecv[n, x] + xrecv[n]

    def attend(head, query):
        keys = kvbuf[:, :, :HD].reshape((back + 1) * rows, HD)
        values = kvbuf[:, :, HD:].reshape((back + 1) * rows, HD)
        scores = (
            lax.dot_general(
                query, keys, (((1,), (1,)), ((), ())), preferred_element_type=jnp.float32
            )
            * (1.0 / math.sqrt(HD))
            + bias[...]
        )
        weights = jnp.exp(scores - jnp.max(scores, axis=1, keepdims=True))
        total = jnp.sum(weights, axis=1, keepdims=True)
        out = jnp.dot(weights.astype(jnp.bfloat16), values, preferred_element_type=jnp.float32)
        outbuf[:, head * HD : (head + 1) * HD] = (out / total).astype(jnp.bfloat16)

    forward(0)
    forward(1)
    own.wait()
    for k in range(3):
        h_copy(k).wait_recv()
    matmul(0)
    c_copy(0).start()
    matmul(1)
    c_copy(1).start()
    cross(0)
    cross(1)
    forward(2)
    kv = finish(0)
    kvbuf[back, :, :HD] = rotate(kv[:, :HD], cosine, sine).astype(jnp.bfloat16)
    kvbuf[back, :, HD:] = kv[:, HD:].astype(jnp.bfloat16)
    each_later(lambda d: kv_copy(d).start())
    matmul(2)
    c_copy(2).start()
    heads = finish(1)
    cross(2)
    each_earlier(lambda d: kv_copy(d).wait_recv())
    for h in range(2):
        attend(h, rotate(heads[:, h * HD : (h + 1) * HD], cosine, sine).astype(jnp.bfloat16))
    heads = finish(2)
    for h in range(2):
        attend(h + 2, rotate(heads[:, h * HD : (h + 1) * HD], cosine, sine).astype(jnp.bfloat16))

    tgt = tgt_row_ref[0:1, :]
    tgt_mat = jnp.transpose(jnp.broadcast_to(tgt, (rows, rows)))
    earlier = (tgt_mat == tgt) & (
        lax.broadcasted_iota(jnp.int32, (rows, rows), 0)
        < lax.broadcasted_iota(jnp.int32, (rows, rows), 1)
    )
    rank = jnp.sum(jnp.where(earlier, 1.0, 0.0), axis=0, keepdims=True).astype(jnp.int32)
    cap = packed_ref.shape[0] // n_dev
    place = tgt * cap + rank
    pick = jnp.where(
        lax.broadcasted_iota(jnp.int32, (packed_ref.shape[0], rows), 0) == place, 1.0, 0.0
    ).astype(jnp.bfloat16)
    packed_ref[...] = jnp.dot(pick, outbuf[...], preferred_element_type=jnp.float32).astype(
        jnp.bfloat16
    )

    each_later(lambda d: d_copy(d).wait_send())
    each_later(lambda d: kv_copy(d).wait_send())
    for k in range(3):
        h_copy(k).wait_send()
    for n in range(NCH):
        for dz in range(nz):
            if dz:
                z_copy(n, dz).wait_send()
            y_copy(n, dz).wait_send()
        c_copy(n).wait_send()
        x_copy(n).wait_send()


def body(hidden, norm_gain, w_qkv, doc_ids, target):
    n_dev = lax.axis_size("ctx")
    rows, width = hidden.shape
    depth = w_qkv.shape[0]
    cap = 2 * rows // n_dev
    back = -(-(MOST - 1) // rows)
    nz = n_dev // 8
    me = lax.axis_index("ctx")
    half = HD // 2
    freqs = 500000.0 ** (-(jnp.arange(half, dtype=jnp.float32) * 2.0) / HD)
    freq_row = jnp.concatenate([freqs, freqs])[None, :]
    doc_row = jnp.broadcast_to(doc_ids[None, :], (8, rows))
    tgt_row = jnp.broadcast_to(target[None, :], (8, rows))
    bf16, f32 = jnp.bfloat16, jnp.float32
    dma = pltpu.SemaphoreType.DMA
    packed = pl.pallas_call(
        functools.partial(kernel, n_dev),
        out_shape=jax.ShapeDtypeStruct((n_dev * cap, QH * HD), bf16),
        in_specs=[pl.BlockSpec(memory_space=pltpu.VMEM)] * 7,
        out_specs=pl.BlockSpec(memory_space=pltpu.VMEM),
        scratch_shapes=[
            pltpu.VMEM((4, rows, width // 4), bf16),
            pltpu.VMEM((4, rows, width // 4), bf16),
            pltpu.VMEM((NCH, width // 4, CW), bf16),
            pltpu.VMEM((NCH, 2, 2, rows, CW), f32),
            pltpu.VMEM((NCH, 2, rows, CW), f32),
            pltpu.VMEM((NCH, rows, CW), f32),
            pltpu.VMEM((NCH, rows, CW), f32),
            pltpu.VMEM((back + 1, rows, 2 * HD), bf16),
            pltpu.VMEM((back + 1, 8, rows), jnp.int32),
            pltpu.VMEM((rows, (back + 1) * rows), f32),
            pltpu.VMEM((rows, QH * HD), bf16),
            dma((3,)), dma((3,)), dma,
            dma((NCH, nz)), dma((NCH, nz)), dma((NCH, nz)), dma((NCH, nz)),
            dma((NCH,)), dma((NCH,)), dma((NCH,)), dma((NCH,)),
            dma((back,)), dma((back,)), dma((back,)), dma((back,)),
        ],
        compiler_params=pltpu.CompilerParams(
            collective_id=0, has_side_effects=True, vmem_limit_bytes=48 * 1024 * 1024
        ),
        cost_estimate=pl.CostEstimate(
            flops=2 * rows * width * 768, bytes_accessed=4 * 1024 * 1024, transcendentals=0
        ),
    )(
        hidden, norm_gain.astype(f32)[None, :], w_qkv, doc_row, doc_ids[:, None], tgt_row, freq_row
    )
    table = lax.all_gather(target, "ctx", axis=0, tiled=False)
    moved = lax.all_to_all(
        packed.reshape(n_dev, cap, QH * HD), "ctx", split_axis=0, concat_axis=0, tiled=True
    )
    counts = jnp.sum((table == me).astype(jnp.int32), axis=1)
    first = jnp.cumsum(counts) - counts
    lane = jnp.arange(cap, dtype=jnp.int32)[None, :]
    dest = jnp.where(lane < counts[:, None], first[:, None] + lane, -1).reshape(-1)
    pick = (jnp.arange(rows, dtype=jnp.int32)[:, None] == dest[None, :]).astype(bf16)
    return jnp.dot(pick, moved.reshape(n_dev * cap, QH * HD), preferred_element_type=f32).astype(bf16)


def solution(mesh):
    in_specs = (
        P(("section", "ctx"), None),
        P(),
        P("ctx", None),
        P(("section", "ctx")),
        P(("section", "ctx")),
    )
    out_specs = P(("section", "ctx"), None)
    return jax.shard_map(body, mesh=mesh, in_specs=in_specs, out_specs=out_specs, check_vma=False)
```

```python
import functools
import math

import jax
import jax.numpy as jnp
import numpy as np
from jax import lax
from jax.experimental import pallas as pl
from jax.experimental.pallas import tpu as pltpu
from jax.sharding import PartitionSpec as P

HD = 128
QH = 4
MOST = 1024
NCH = 3
CW = 256
COLS = (2, 0, 1)
PLACE = (0, 2, 1, 3)
MESH = pl.DeviceIdType.MESH


def rotate(block, cosine, sine):
    return block * cosine + pltpu.roll(block, HD // 2, 1) * sine


def kernel(
    n_dev, hidden_hbm, gain_ref, w_hbm, doc_ref, tgt_ref, freq_ref, result_ref,
    hidden_ref, gain32, nsend, xg, wbuf, part, crecv, xsend, xrecv, kvbuf, ids, bias, outbuf, abuf, rbuf,
    load_sem, w_sem,
    h_send, h_recv, h_own, z_send, z_recv, y_send, y_recv, c_send, c_recv, x_send, x_recv,
    kv_send, kv_recv, i_send, i_recv, a_send, a_recv,
):
    rows = hidden_ref.shape[0]
    depth = w_hbm.shape[0]
    width = hidden_ref.shape[1]
    back = kvbuf.shape[0] - 1
    nz = n_dev // 8
    shards = n_dev // 4
    me = lax.axis_index("ctx")
    z, y, x, c = me // 8, (me // 4) % 2, (me // 2) % 2, me % 2
    spot = 2 * c + x
    shard = me // 4

    def remote(src, dst, send, recv, dev):
        return pltpu.make_async_remote_copy(
            src_ref=src, dst_ref=dst, send_sem=send, recv_sem=recv,
            device_id={"ctx": dev}, device_id_type=MESH,
        )

    def slot(n, j):
        return wbuf.at[n, pl.ds(pl.multiple_of(j * depth, depth), depth), :]

    def w_load(n):
        return pltpu.make_async_copy(
            w_hbm.at[:, COLS[n] * CW : (COLS[n] + 1) * CW], slot(n, shard), w_sem.at[n]
        )

    for n in range(NCH):
        w_load(n).start()
    load = pltpu.make_async_copy(hidden_hbm, hidden_ref, load_sem)
    load.start()
    doc = doc_ref[...]
    tgt = tgt_ref[...]
    ids[me] = jnp.where(
        lax.broadcasted_iota(jnp.int32, (8, rows), 0) == 0,
        jnp.broadcast_to(doc, (8, rows)),
        jnp.broadcast_to(tgt, (8, rows)),
    )

    barrier = pltpu.get_barrier_semaphore()

    def greet(d, carry):
        pl.semaphore_signal(
            barrier, inc=1, device_id={"ctx": lax.rem(me + d, n_dev)}, device_id_type=MESH
        )
        return carry

    lax.fori_loop(1, n_dev, greet, 0)
    gain32[...] = gain_ref[...].astype(jnp.float32)
    kvbuf[...] = jnp.zeros_like(kvbuf)
    pl.semaphore_wait(barrier, n_dev - 1)

    y_dev = z * 8 + (1 - y) * 4 + x * 2 + c
    c_dev = z * 8 + y * 4 + x * 2 + (1 - c)
    x_dev = z * 8 + y * 4 + (1 - x) * 2 + c

    def y_copy(n, dz):
        j = lax.rem(z - dz + nz, nz) * 2 + y
        return remote(slot(n, j), slot(n, j), y_send.at[n, dz], y_recv.at[n, dz], y_dev)

    def z_copy(n, dz):
        dev = lax.rem(z + dz, nz) * 8 + y * 4 + x * 2 + c
        return remote(slot(n, shard), slot(n, shard), z_send.at[n, dz], z_recv.at[n, dz], dev)

    def i_copy(d):
        return remote(ids.at[me], ids.at[me], i_send.at[d], i_recv.at[d], lax.rem(me + d, n_dev))

    def a_copy(d):
        dev = lax.rem(me + d, n_dev)
        return remote(abuf.at[dev], rbuf.at[me], a_send.at[d], a_recv.at[d], dev)

    def each_other(do):
        def one(d, carry):
            do(d)
            return carry

        lax.fori_loop(1, n_dev, one, 0)

    def kv_copy(d):
        return remote(
            kvbuf.at[back], kvbuf.at[back - d], kv_send.at[d - 1], kv_recv.at[d - 1],
            lax.rem(me + d, n_dev),
        )

    def each_later(do):
        for d in range(1, back + 1):
            pl.when(me + d < n_dev)(functools.partial(do, d))

    def each_earlier(do):
        for d in range(1, back + 1):
            pl.when(me >= d)(functools.partial(do, d))

    for n in range(NCH):
        w_load(n).wait()
        for dz in range(nz):
            if dz:
                z_copy(n, dz).start()
            else:
                y_copy(n, 0).start()
        if n == 0:
            each_other(lambda d: i_copy(d).start())
    load.wait()

    step = 16

    def norm_rows(i, carry):
        at = pl.ds(pl.multiple_of(i * step, step), step)
        total = jnp.zeros((step, CW), jnp.float32)
        for b in range(width // CW):
            v = hidden_ref[at, b * CW : (b + 1) * CW].astype(jnp.float32)
            total = total + v * v
        scale = lax.rsqrt(jnp.sum(total, axis=1, keepdims=True) * (1.0 / width) + 1e-05)
        for b in range(width // depth):
            v = hidden_ref[at, b * depth : (b + 1) * depth].astype(jnp.float32)
            g = gain32[:, b * depth : (b + 1) * depth]
            nsend[PLACE[b % 4], at, (b // 4) * depth : (b // 4 + 1) * depth] = (
                v * scale * g
            ).astype(jnp.bfloat16)
        return carry

    lax.fori_loop(0, rows // step, norm_rows, 0)

    def h_copy(k):
        dx, dc = ((1, 0), (1, 1), (0, 1))[k]
        ox = 1 - x if dx else x
        oc = 1 - c if dc else c
        return remote(
            nsend.at[2 * oc + ox], xg.at[spot], h_send.at[k], h_recv.at[k],
            z * 8 + y * 4 + ox * 2 + oc,
        )

    for k in range(3):
        h_copy(k).start()
    own = pltpu.make_async_copy(nsend.at[spot], xg.at[spot], h_own)
    own.start()

    def forward(n):
        for dz in range(1, nz):
            z_copy(n, dz).wait_recv()
            y_copy(n, dz).start()

    def matmul(n):
        for dz in range(nz):
            y_copy(n, dz).wait_recv()
        left = xg[...].reshape(4 * rows, xg.shape[2])
        part[n] = jnp.dot(left, wbuf[n], preferred_element_type=jnp.float32).reshape(
            2, 2, rows, CW
        )

    def c_copy(n):
        return remote(part.at[n, 1 - c], crecv.at[n], c_send.at[n], c_recv.at[n], c_dev)

    def x_copy(n):
        return remote(xsend.at[n], xrecv.at[n], x_send.at[n], x_recv.at[n], x_dev)

    def cross(n):
        c_copy(n).wait_recv()
        xsend[n] = part[n, c, 1 - x] + crecv[n, 1 - x]
        x_copy(n).start()

    def finish(n):
        x_copy(n).wait_recv()
        return part[n, c, x] + crecv[n, x] + xrecv[n]

    def attend(head, query):
        keys = kvbuf[:, :, :HD].reshape((back + 1) * rows, HD)
        values = kvbuf[:, :, HD:].reshape((back + 1) * rows, HD)
        scores = (
            lax.dot_general(
                query, keys, (((1,), (1,)), ((), ())), preferred_element_type=jnp.float32
            )
            * (1.0 / math.sqrt(HD))
            + bias[...]
        )
        weights = jnp.exp(scores - jnp.max(scores, axis=1, keepdims=True))
        total = jnp.sum(weights, axis=1, keepdims=True)
        out = jnp.dot(weights.astype(jnp.bfloat16), values, preferred_element_type=jnp.float32)
        outbuf[:, head * HD : (head + 1) * HD] = (out / total).astype(jnp.bfloat16)

    forward(0)
    each_other(lambda d: i_copy(d).wait_recv())
    doc_col = jnp.transpose(jnp.broadcast_to(doc, (rows, rows)))
    count = jnp.zeros((rows, 1), jnp.float32)
    for s in range(back + 1):
        near = ids[lax.rem(me + n_dev - back + s, n_dev), 0:1, :]
        seen = doc_col == jnp.where(me + s >= back, near, -1)
        if s == back:
            seen = seen & (
                lax.broadcasted_iota(jnp.int32, (rows, rows), 1)
                <= lax.broadcasted_iota(jnp.int32, (rows, rows), 0)
            )
        bias[:, s * rows : (s + 1) * rows] = jnp.where(seen, 0.0, -1e30)
        count = count + jnp.sum(jnp.where(seen, 1.0, 0.0), axis=1, keepdims=True)
    angle = (count - 1.0) * freq_ref[...]
    cosine = jnp.cos(angle)
    sine = jnp.sin(angle) * jnp.where(
        lax.broadcasted_iota(jnp.int32, (rows, HD), 1) < HD // 2, -1.0, 1.0
    )

    forward(1)
    own.wait()
    for k in range(3):
        h_copy(k).wait_recv()
    matmul(0)
    c_copy(0).start()
    matmul(1)
    c_copy(1).start()
    cross(0)
    cross(1)
    forward(2)
    kv = finish(0)
    kvbuf[back, :, :HD] = rotate(kv[:, :HD], cosine, sine).astype(jnp.bfloat16)
    kvbuf[back, :, HD:] = kv[:, HD:].astype(jnp.bfloat16)
    each_later(lambda d: kv_copy(d).start())
    matmul(2)
    c_copy(2).start()
    heads = finish(1)
    cross(2)
    each_earlier(lambda d: kv_copy(d).wait_recv())
    for h in range(2):
        attend(h, rotate(heads[:, h * HD : (h + 1) * HD], cosine, sine).astype(jnp.bfloat16))
    heads = finish(2)
    for h in range(2):
        attend(h + 2, rotate(heads[:, h * HD : (h + 1) * HD], cosine, sine).astype(jnp.bfloat16))

    tgt_mat = jnp.transpose(jnp.broadcast_to(tgt, (rows, rows)))
    earlier = (tgt_mat == tgt) & (
        lax.broadcasted_iota(jnp.int32, (rows, rows), 0)
        < lax.broadcasted_iota(jnp.int32, (rows, rows), 1)
    )
    rank = jnp.sum(jnp.where(earlier, 1.0, 0.0), axis=0, keepdims=True).astype(jnp.int32)
    cap = abuf.shape[1] // 2
    slots = n_dev * 2 * cap
    slot_col = lax.broadcasted_iota(jnp.int32, (slots, rows), 0)
    place = tgt * (2 * cap) + rank
    half = QH * HD // 2
    packed = jnp.dot(
        jnp.where(slot_col == place, 1.0, 0.0).astype(jnp.bfloat16),
        outbuf[:, :half],
        preferred_element_type=jnp.float32,
    ) + jnp.dot(
        jnp.where(slot_col == place + cap, 1.0, 0.0).astype(jnp.bfloat16),
        outbuf[:, half:],
        preferred_element_type=jnp.float32,
    )
    abuf[...] = packed.astype(jnp.bfloat16).reshape(abuf.shape)
    each_other(lambda d: a_copy(d).start())
    rbuf[me] = abuf[me]

    counts = jnp.sum(jnp.where(ids[:, 1, :] == me, 1.0, 0.0), axis=1, keepdims=True)
    lane = lax.broadcasted_iota(jnp.int32, (n_dev, slots), 1)
    source = lax.broadcasted_iota(jnp.int32, (n_dev, slots), 0)
    owner = lane // (2 * cap)
    count_row = jnp.sum(jnp.where(source == owner, counts, 0.0), axis=0, keepdims=True)
    first_row = jnp.sum(jnp.where(source < owner, counts, 0.0), axis=0, keepdims=True)
    inner = lax.broadcasted_iota(jnp.int32, (1, slots), 1) % (2 * cap)
    index = inner % cap
    goal = jnp.where(
        index < count_row.astype(jnp.int32), first_row.astype(jnp.int32) + index, -1
    )
    out_row = lax.broadcasted_iota(jnp.int32, (rows, slots), 0)
    picks = [
        jnp.where(out_row == jnp.where(inner // cap == h, goal, -1), 1.0, 0.0).astype(jnp.bfloat16)
        for h in range(2)
    ]
    each_other(lambda d: a_copy(d).wait_recv())
    arrived = rbuf[...].reshape(slots, half)
    for h in range(2):
        result_ref[:, h * half : (h + 1) * half] = jnp.dot(
            picks[h], arrived, preferred_element_type=jnp.float32
        ).astype(jnp.bfloat16)

    each_other(lambda d: i_copy(d).wait_send())
    each_other(lambda d: a_copy(d).wait_send())
    each_later(lambda d: kv_copy(d).wait_send())
    for k in range(3):
        h_copy(k).wait_send()
    for n in range(NCH):
        for dz in range(nz):
            if dz:
                z_copy(n, dz).wait_send()
            y_copy(n, dz).wait_send()
        c_copy(n).wait_send()
        x_copy(n).wait_send()


def body(hidden, norm_gain, w_qkv, doc_ids, target):
    n_dev = lax.axis_size("ctx")
    rows, width = hidden.shape
    depth = w_qkv.shape[0]
    cap = 2 * rows // n_dev
    back = -(-(MOST - 1) // rows)
    nz = n_dev // 8
    freqs = 500000.0 ** (-(np.arange(HD // 2, dtype=np.float64) * 2.0) / HD)
    freq_row = jnp.asarray(np.concatenate([freqs, freqs])[None, :], jnp.float32)
    bf16, f32 = jnp.bfloat16, jnp.float32
    dma = pltpu.SemaphoreType.DMA
    return pl.pallas_call(
        functools.partial(kernel, n_dev),
        out_shape=jax.ShapeDtypeStruct((rows, QH * HD), bf16),
        in_specs=[
            pl.BlockSpec(memory_space=pltpu.HBM if i in (0, 2) else pltpu.VMEM) for i in range(6)
        ],
        out_specs=pl.BlockSpec(memory_space=pltpu.VMEM),
        scratch_shapes=[
            pltpu.VMEM((rows, width), bf16),
            pltpu.VMEM((1, width), f32),
            pltpu.VMEM((4, rows, width // 4), bf16),
            pltpu.VMEM((4, rows, width // 4), bf16),
            pltpu.VMEM((NCH, width // 4, CW), bf16),
            pltpu.VMEM((NCH, 2, 2, rows, CW), f32),
            pltpu.VMEM((NCH, 2, rows, CW), f32),
            pltpu.VMEM((NCH, rows, CW), f32),
            pltpu.VMEM((NCH, rows, CW), f32),
            pltpu.VMEM((back + 1, rows, 2 * HD), bf16),
            pltpu.VMEM((n_dev, 8, rows), jnp.int32),
            pltpu.VMEM((rows, (back + 1) * rows), f32),
            pltpu.VMEM((rows, QH * HD), bf16),
            pltpu.VMEM((n_dev, 2 * cap, QH * HD // 2), bf16),
            pltpu.VMEM((n_dev, 2 * cap, QH * HD // 2), bf16),
            dma, dma((NCH,)),
            dma((3,)), dma((3,)), dma,
            dma((NCH, nz)), dma((NCH, nz)), dma((NCH, nz)), dma((NCH, nz)),
            dma((NCH,)), dma((NCH,)), dma((NCH,)), dma((NCH,)),
            dma((back,)), dma((back,)), dma((n_dev,)), dma((n_dev,)), dma((n_dev,)), dma((n_dev,)),
        ],
        compiler_params=pltpu.CompilerParams(
            collective_id=0, has_side_effects=True, vmem_limit_bytes=63 * 1024 * 1024
        ),
        cost_estimate=pl.CostEstimate(
            flops=2 * rows * width * 768, bytes_accessed=4 * 1024 * 1024, transcendentals=0
        ),
    )(
        hidden, norm_gain[None, :], w_qkv, doc_ids[None, :], target[None, :], freq_row
    )


def solution(mesh):
    in_specs = (
        P(("section", "ctx"), None),
        P(),
        P("ctx", None),
        P(("section", "ctx")),
        P(("section", "ctx")),
    )
    out_specs = P(("section", "ctx"), None)
    return jax.shard_map(body, mesh=mesh, in_specs=in_specs, out_specs=out_specs, check_vma=False)
```

```python
import functools
import math

import jax
import jax.numpy as jnp
import numpy as np
from jax import lax
from jax.experimental import pallas as pl
from jax.experimental.pallas import tpu as pltpu
from jax.sharding import PartitionSpec as P

HD = 128
QH = 4
MOST = 1024
NCH = 3
CW = 256
COLS = (2, 0, 1)
PLACE = (0, 2, 1, 3)
MESH = pl.DeviceIdType.MESH


def rotate(block, cosine, sine):
    return block * cosine + pltpu.roll(block, HD // 2, 1) * sine


def kernel(
    n_dev, hidden_hbm, gain_ref, w_hbm, doc_ref, tgt_ref, freq_ref, result_ref,
    hidden_ref, gain32, nsend, xg, wbuf, part, crecv, xsend, xrecv, kvbuf, ids, bias, outbuf, abuf, rbuf,
    load_sem, w_sem,
    h_send, h_recv, h_own, z_send, z_recv, y_send, y_recv, c_send, c_recv, x_send, x_recv,
    kv_send, kv_recv, i_send, i_recv, a_send, a_recv,
):
    rows = hidden_ref.shape[0]
    depth = w_hbm.shape[0]
    width = hidden_ref.shape[1]
    back = kvbuf.shape[0] - 1
    nz = n_dev // 8
    shards = n_dev // 4
    me = lax.axis_index("ctx")
    z, y, x, c = me // 8, (me // 4) % 2, (me // 2) % 2, me % 2
    spot = 2 * c + x
    shard = me // 4

    def remote(src, dst, send, recv, dev):
        return pltpu.make_async_remote_copy(
            src_ref=src, dst_ref=dst, send_sem=send, recv_sem=recv,
            device_id={"ctx": dev}, device_id_type=MESH,
        )

    def slot(n, j):
        return wbuf.at[n, pl.ds(pl.multiple_of(j * depth, depth), depth), :]

    def w_load(n):
        return pltpu.make_async_copy(
            w_hbm.at[:, COLS[n] * CW : (COLS[n] + 1) * CW], slot(n, shard), w_sem.at[n]
        )

    for n in range(NCH):
        w_load(n).start()
    load = pltpu.make_async_copy(hidden_hbm, hidden_ref, load_sem)
    load.start()
    doc = doc_ref[...]
    tgt = tgt_ref[...]
    ids[me] = jnp.where(
        lax.broadcasted_iota(jnp.int32, (8, rows), 0) == 0,
        jnp.broadcast_to(doc, (8, rows)),
        jnp.broadcast_to(tgt, (8, rows)),
    )

    barrier = pltpu.get_barrier_semaphore()

    def greet(d, carry):
        pl.semaphore_signal(
            barrier, inc=1, device_id={"ctx": lax.rem(me + d, n_dev)}, device_id_type=MESH
        )
        return carry

    lax.fori_loop(1, n_dev, greet, 0)
    gain32[...] = gain_ref[...].astype(jnp.float32)
    kvbuf[...] = jnp.zeros_like(kvbuf)
    pl.semaphore_wait(barrier, n_dev - 1)

    y_dev = z * 8 + (1 - y) * 4 + x * 2 + c
    c_dev = z * 8 + y * 4 + x * 2 + (1 - c)
    x_dev = z * 8 + y * 4 + (1 - x) * 2 + c

    def y_copy(n, zs):
        j = zs * 2 + y
        return remote(slot(n, j), slot(n, j), y_send.at[n, zs], y_recv.at[n, zs], y_dev)

    def z_copy(n, zs, way):
        j = zs * 2 + y
        send = z_send.at[n, zs, (way + 1) // 2]
        return remote(slot(n, j), slot(n, j), send, z_recv.at[n, zs], me + 8 * way)

    def z_own(n):
        pl.when(z < nz - 1)(lambda: z_copy(n, z, 1).start())
        pl.when(z > 0)(lambda: z_copy(n, z, -1).start())

    def pass_on(n, k, way):
        zs = z - k * way
        last = z == (nz - 1 if way > 0 else 0)

        @pl.when((zs >= 0) & (zs < nz))
        def _():
            z_copy(n, zs, way).wait_recv()
            pl.when(jnp.logical_not(last))(lambda: z_copy(n, zs, way).start())
            y_copy(n, zs).start()

    def z_left(n, k, way):
        zs = z - k * way
        last = z == (nz - 1 if way > 0 else 0)
        pl.when((zs >= 0) & (zs < nz) & jnp.logical_not(last))(
            lambda: z_copy(n, zs, way).wait_send()
        )

    def i_copy(d):
        return remote(ids.at[me], ids.at[me], i_send.at[d], i_recv.at[d], lax.rem(me + d, n_dev))

    def a_copy(d):
        dev = lax.rem(me + d, n_dev)
        return remote(abuf.at[dev], rbuf.at[me], a_send.at[d], a_recv.at[d], dev)

    def each_other(do):
        def one(d, carry):
            do(d)
            return carry

        lax.fori_loop(1, n_dev, one, 0)

    def kv_copy(d):
        return remote(
            kvbuf.at[back], kvbuf.at[back - d], kv_send.at[d - 1], kv_recv.at[d - 1],
            lax.rem(me + d, n_dev),
        )

    def each_later(do):
        for d in range(1, back + 1):
            pl.when(me + d < n_dev)(functools.partial(do, d))

    def each_earlier(do):
        for d in range(1, back + 1):
            pl.when(me >= d)(functools.partial(do, d))

    for n in range(NCH):
        w_load(n).wait()
        if n == 0:
            z_own(n)
            y_copy(n, z).start()
            each_other(lambda d: i_copy(d).start())
    load.wait()

    step = 16

    def norm_rows(i, carry):
        at = pl.ds(pl.multiple_of(i * step, step), step)
        total = jnp.zeros((step, CW), jnp.float32)
        for b in range(width // CW):
            v = hidden_ref[at, b * CW : (b + 1) * CW].astype(jnp.float32)
            total = total + v * v
        scale = lax.rsqrt(jnp.sum(total, axis=1, keepdims=True) * (1.0 / width) + 1e-05)
        for b in range(width // depth):
            v = hidden_ref[at, b * depth : (b + 1) * depth].astype(jnp.float32)
            g = gain32[:, b * depth : (b + 1) * depth]
            nsend[PLACE[b % 4], at, (b // 4) * depth : (b // 4 + 1) * depth] = (
                v * scale * g
            ).astype(jnp.bfloat16)
        return carry

    lax.fori_loop(0, rows // step, norm_rows, 0)

    def h_copy(k):
        dx, dc = ((1, 0), (1, 1), (0, 1))[k]
        ox = 1 - x if dx else x
        oc = 1 - c if dc else c
        return remote(
            nsend.at[2 * oc + ox], xg.at[spot], h_send.at[k], h_recv.at[k],
            z * 8 + y * 4 + ox * 2 + oc,
        )

    for k in range(3):
        h_copy(k).start()
    own = pltpu.make_async_copy(nsend.at[spot], xg.at[spot], h_own)
    own.start()

    def forward(n):
        for k in range(1, nz):
            for way in (1, -1):
                pass_on(n, k, way)
            if k == 1 and n + 1 < NCH:
                z_own(n + 1)
        if n + 1 < NCH:
            y_copy(n + 1, z).start()

    def matmul(n):
        for dz in range(nz):
            y_copy(n, dz).wait_recv()
        left = xg[...].reshape(4 * rows, xg.shape[2])
        part[n] = jnp.dot(left, wbuf[n], preferred_element_type=jnp.float32).reshape(
            2, 2, rows, CW
        )

    def c_copy(n):
        return remote(part.at[n, 1 - c], crecv.at[n], c_send.at[n], c_recv.at[n], c_dev)

    def x_copy(n):
        return remote(xsend.at[n], xrecv.at[n], x_send.at[n], x_recv.at[n], x_dev)

    def cross(n):
        c_copy(n).wait_recv()
        xsend[n] = part[n, c, 1 - x] + crecv[n, 1 - x]
        x_copy(n).start()

    def finish(n):
        x_copy(n).wait_recv()
        return part[n, c, x] + crecv[n, x] + xrecv[n]

    def attend(head, query):
        keys = kvbuf[:, :, :HD].reshape((back + 1) * rows, HD)
        values = kvbuf[:, :, HD:].reshape((back + 1) * rows, HD)
        scores = (
            lax.dot_general(
                query, keys, (((1,), (1,)), ((), ())), preferred_element_type=jnp.float32
            )
            * (1.0 / math.sqrt(HD))
            + bias[...]
        )
        weights = jnp.exp(scores - jnp.max(scores, axis=1, keepdims=True))
        total = jnp.sum(weights, axis=1, keepdims=True)
        out = jnp.dot(weights.astype(jnp.bfloat16), values, preferred_element_type=jnp.float32)
        outbuf[:, head * HD : (head + 1) * HD] = (out / total).astype(jnp.bfloat16)

    forward(0)
    each_other(lambda d: i_copy(d).wait_recv())
    doc_col = jnp.transpose(jnp.broadcast_to(doc, (rows, rows)))
    count = jnp.zeros((rows, 1), jnp.float32)
    for s in range(back + 1):
        near = ids[lax.rem(me + n_dev - back + s, n_dev), 0:1, :]
        seen = doc_col == jnp.where(me + s >= back, near, -1)
        if s == back:
            seen = seen & (
                lax.broadcasted_iota(jnp.int32, (rows, rows), 1)
                <= lax.broadcasted_iota(jnp.int32, (rows, rows), 0)
            )
        bias[:, s * rows : (s + 1) * rows] = jnp.where(seen, 0.0, -1e30)
        count = count + jnp.sum(jnp.where(seen, 1.0, 0.0), axis=1, keepdims=True)
    angle = (count - 1.0) * freq_ref[...]
    cosine = jnp.cos(angle)
    sine = jnp.sin(angle) * jnp.where(
        lax.broadcasted_iota(jnp.int32, (rows, HD), 1) < HD // 2, -1.0, 1.0
    )

    forward(1)
    forward(2)
    own.wait()
    for k in range(3):
        h_copy(k).wait_recv()
    matmul(0)
    c_copy(0).start()
    matmul(1)
    c_copy(1).start()
    cross(0)
    kv = finish(0)
    kvbuf[back, :, :HD] = rotate(kv[:, :HD], cosine, sine).astype(jnp.bfloat16)
    kvbuf[back, :, HD:] = kv[:, HD:].astype(jnp.bfloat16)
    each_later(lambda d: kv_copy(d).start())
    cross(1)
    matmul(2)
    c_copy(2).start()
    heads = finish(1)
    cross(2)
    each_earlier(lambda d: kv_copy(d).wait_recv())
    for h in range(2):
        attend(h, rotate(heads[:, h * HD : (h + 1) * HD], cosine, sine).astype(jnp.bfloat16))
    heads = finish(2)
    for h in range(2):
        attend(h + 2, rotate(heads[:, h * HD : (h + 1) * HD], cosine, sine).astype(jnp.bfloat16))

    tgt_mat = jnp.transpose(jnp.broadcast_to(tgt, (rows, rows)))
    earlier = (tgt_mat == tgt) & (
        lax.broadcasted_iota(jnp.int32, (rows, rows), 0)
        < lax.broadcasted_iota(jnp.int32, (rows, rows), 1)
    )
    rank = jnp.sum(jnp.where(earlier, 1.0, 0.0), axis=0, keepdims=True).astype(jnp.int32)
    cap = abuf.shape[1] // 2
    slots = n_dev * 2 * cap
    slot_col = lax.broadcasted_iota(jnp.int32, (slots, rows), 0)
    place = tgt * (2 * cap) + rank
    half = QH * HD // 2
    packed = jnp.dot(
        jnp.where(slot_col == place, 1.0, 0.0).astype(jnp.bfloat16),
        outbuf[:, :half],
        preferred_element_type=jnp.float32,
    ) + jnp.dot(
        jnp.where(slot_col == place + cap, 1.0, 0.0).astype(jnp.bfloat16),
        outbuf[:, half:],
        preferred_element_type=jnp.float32,
    )
    abuf[...] = packed.astype(jnp.bfloat16).reshape(abuf.shape)
    each_other(lambda d: a_copy(d).start())
    rbuf[me] = abuf[me]

    counts = jnp.sum(jnp.where(ids[:, 1, :] == me, 1.0, 0.0), axis=1, keepdims=True)
    lane = lax.broadcasted_iota(jnp.int32, (n_dev, slots), 1)
    source = lax.broadcasted_iota(jnp.int32, (n_dev, slots), 0)
    owner = lane // (2 * cap)
    count_row = jnp.sum(jnp.where(source == owner, counts, 0.0), axis=0, keepdims=True)
    first_row = jnp.sum(jnp.where(source < owner, counts, 0.0), axis=0, keepdims=True)
    inner = lax.broadcasted_iota(jnp.int32, (1, slots), 1) % (2 * cap)
    index = inner % cap
    goal = jnp.where(
        index < count_row.astype(jnp.int32), first_row.astype(jnp.int32) + index, -1
    )
    out_row = lax.broadcasted_iota(jnp.int32, (rows, slots), 0)
    picks = [
        jnp.where(out_row == jnp.where(inner // cap == h, goal, -1), 1.0, 0.0).astype(jnp.bfloat16)
        for h in range(2)
    ]
    each_other(lambda d: a_copy(d).wait_recv())
    arrived = rbuf[...].reshape(slots, half)
    for h in range(2):
        result_ref[:, h * half : (h + 1) * half] = jnp.dot(
            picks[h], arrived, preferred_element_type=jnp.float32
        ).astype(jnp.bfloat16)

    each_other(lambda d: i_copy(d).wait_send())
    each_other(lambda d: a_copy(d).wait_send())
    each_later(lambda d: kv_copy(d).wait_send())
    for k in range(3):
        h_copy(k).wait_send()
    for n in range(NCH):
        for dz in range(nz):
            for way in (1, -1):
                z_left(n, dz, way)
            y_copy(n, dz).wait_send()
        c_copy(n).wait_send()
        x_copy(n).wait_send()


def body(hidden, norm_gain, w_qkv, doc_ids, target):
    n_dev = lax.axis_size("ctx")
    rows, width = hidden.shape
    depth = w_qkv.shape[0]
    cap = 2 * rows // n_dev
    back = -(-(MOST - 1) // rows)
    nz = n_dev // 8
    freqs = 500000.0 ** (-(np.arange(HD // 2, dtype=np.float64) * 2.0) / HD)
    freq_row = jnp.asarray(np.concatenate([freqs, freqs])[None, :], jnp.float32)
    bf16, f32 = jnp.bfloat16, jnp.float32
    dma = pltpu.SemaphoreType.DMA
    return pl.pallas_call(
        functools.partial(kernel, n_dev),
        out_shape=jax.ShapeDtypeStruct((rows, QH * HD), bf16),
        in_specs=[
            pl.BlockSpec(memory_space=pltpu.HBM if i in (0, 2) else pltpu.VMEM) for i in range(6)
        ],
        out_specs=pl.BlockSpec(memory_space=pltpu.VMEM),
        scratch_shapes=[
            pltpu.VMEM((rows, width), bf16),
            pltpu.VMEM((1, width), f32),
            pltpu.VMEM((4, rows, width // 4), bf16),
            pltpu.VMEM((4, rows, width // 4), bf16),
            pltpu.VMEM((NCH, width // 4, CW), bf16),
            pltpu.VMEM((NCH, 2, 2, rows, CW), f32),
            pltpu.VMEM((NCH, 2, rows, CW), f32),
            pltpu.VMEM((NCH, rows, CW), f32),
            pltpu.VMEM((NCH, rows, CW), f32),
            pltpu.VMEM((back + 1, rows, 2 * HD), bf16),
            pltpu.VMEM((n_dev, 8, rows), jnp.int32),
            pltpu.VMEM((rows, (back + 1) * rows), f32),
            pltpu.VMEM((rows, QH * HD), bf16),
            pltpu.VMEM((n_dev, 2 * cap, QH * HD // 2), bf16),
            pltpu.VMEM((n_dev, 2 * cap, QH * HD // 2), bf16),
            dma, dma((NCH,)),
            dma((3,)), dma((3,)), dma,
            dma((NCH, nz, 2)), dma((NCH, nz)), dma((NCH, nz)), dma((NCH, nz)),
            dma((NCH,)), dma((NCH,)), dma((NCH,)), dma((NCH,)),
            dma((back,)), dma((back,)), dma((n_dev,)), dma((n_dev,)), dma((n_dev,)), dma((n_dev,)),
        ],
        compiler_params=pltpu.CompilerParams(
            collective_id=0, has_side_effects=True, vmem_limit_bytes=63 * 1024 * 1024
        ),
        cost_estimate=pl.CostEstimate(
            flops=2 * rows * width * 768, bytes_accessed=4 * 1024 * 1024, transcendentals=0
        ),
    )(
        hidden, norm_gain[None, :], w_qkv, doc_ids[None, :], target[None, :], freq_row
    )


def solution(mesh):
    in_specs = (
        P(("section", "ctx"), None),
        P(),
        P("ctx", None),
        P(("section", "ctx")),
        P(("section", "ctx")),
    )
    out_specs = P(("section", "ctx"), None)
    return jax.shard_map(body, mesh=mesh, in_specs=in_specs, out_specs=out_specs, check_vma=False)
```

```python
import functools
import math

import jax
import jax.numpy as jnp
import numpy as np
from jax import lax
from jax.experimental import pallas as pl
from jax.experimental.pallas import tpu as pltpu
from jax.sharding import PartitionSpec as P

HD = 128
QH = 4
MOST = 1024
NCH = 3
CW = 256
COLS = (2, 0, 1)
PLACE = (0, 2, 1, 3)
MESH = pl.DeviceIdType.MESH


def rotate(block, cosine, sine):
    return block * cosine + pltpu.roll(block, HD // 2, 1) * sine


def kernel(
    n_dev, hidden_hbm, gain_ref, w_hbm, doc_ref, tgt_ref, freq_ref, result_ref,
    hidden_ref, gain32, nsend, xg, wbuf, part, crecv, xsend, xrecv, kvbuf, ids, bias, outbuf, abuf, rbuf,
    load_sem, w_sem,
    h_send, h_recv, h_own, z_send, z_recv, y_send, y_recv, c_send, c_recv, x_send, x_recv,
    kv_send, kv_recv, i_send, i_recv, a_send, a_recv,
):
    rows = hidden_ref.shape[0]
    depth = w_hbm.shape[0]
    width = hidden_ref.shape[1]
    back = kvbuf.shape[0] - 1
    nz = n_dev // 8
    shards = n_dev // 4
    me = lax.axis_index("ctx")
    z, y, x, c = me // 8, (me // 4) % 2, (me // 2) % 2, me % 2
    spot = 2 * c + x
    shard = me // 4

    def remote(src, dst, send, recv, dev):
        return pltpu.make_async_remote_copy(
            src_ref=src, dst_ref=dst, send_sem=send, recv_sem=recv,
            device_id={"ctx": dev}, device_id_type=MESH,
        )

    def slot(n, j):
        return wbuf.at[n, pl.ds(pl.multiple_of(j * depth, depth), depth), :]

    def w_load(n):
        return pltpu.make_async_copy(
            w_hbm.at[:, COLS[n] * CW : (COLS[n] + 1) * CW], slot(n, shard), w_sem.at[n]
        )

    for n in range(NCH):
        w_load(n).start()
    load = pltpu.make_async_copy(hidden_hbm, hidden_ref, load_sem)
    load.start()
    doc = doc_ref[...]
    tgt = tgt_ref[...]
    ids[me] = jnp.where(
        lax.broadcasted_iota(jnp.int32, (8, rows), 0) == 0,
        jnp.broadcast_to(doc, (8, rows)),
        jnp.broadcast_to(tgt, (8, rows)),
    )

    barrier = pltpu.get_barrier_semaphore()

    def greet(d, carry):
        pl.semaphore_signal(
            barrier, inc=1, device_id={"ctx": lax.rem(me + d, n_dev)}, device_id_type=MESH
        )
        return carry

    lax.fori_loop(1, n_dev, greet, 0)
    gain32[...] = gain_ref[...].astype(jnp.float32)
    kvbuf[...] = jnp.zeros_like(kvbuf)
    pl.semaphore_wait(barrier, n_dev - 1)

    y_dev = z * 8 + (1 - y) * 4 + x * 2 + c
    c_dev = z * 8 + y * 4 + x * 2 + (1 - c)
    x_dev = z * 8 + y * 4 + (1 - x) * 2 + c

    def y_copy(n, zs):
        j = zs * 2 + y
        return remote(slot(n, j), slot(n, j), y_send.at[n, zs], y_recv.at[n, zs], y_dev)

    def z_copy(n, zs, way):
        j = zs * 2 + y
        send = z_send.at[n, zs, (way + 1) // 2]
        return remote(slot(n, j), slot(n, j), send, z_recv.at[n, zs], me + 8 * way)

    def z_own(n):
        pl.when(z < nz - 1)(lambda: z_copy(n, z, 1).start())
        pl.when(z > 0)(lambda: z_copy(n, z, -1).start())

    def pass_on(n, k, way):
        zs = z - k * way
        last = z == (nz - 1 if way > 0 else 0)

        @pl.when((zs >= 0) & (zs < nz))
        def _():
            z_copy(n, zs, way).wait_recv()
            pl.when(jnp.logical_not(last))(lambda: z_copy(n, zs, way).start())
            y_copy(n, zs).start()

    def z_left(n, k, way):
        zs = z - k * way
        last = z == (nz - 1 if way > 0 else 0)
        pl.when((zs >= 0) & (zs < nz) & jnp.logical_not(last))(
            lambda: z_copy(n, zs, way).wait_send()
        )

    def i_copy(d):
        return remote(ids.at[me], ids.at[me], i_send.at[d], i_recv.at[d], lax.rem(me + d, n_dev))

    def a_copy(d):
        dev = lax.rem(me + d, n_dev)
        return remote(abuf.at[dev], rbuf.at[me], a_send.at[d], a_recv.at[d], dev)

    def each_other(do):
        def one(d, carry):
            do(d)
            return carry

        lax.fori_loop(1, n_dev, one, 0)

    def kv_copy(d):
        return remote(
            kvbuf.at[back], kvbuf.at[back - d], kv_send.at[d - 1], kv_recv.at[d - 1],
            lax.rem(me + d, n_dev),
        )

    def each_later(do):
        for d in range(1, back + 1):
            pl.when(me + d < n_dev)(functools.partial(do, d))

    def each_earlier(do):
        for d in range(1, back + 1):
            pl.when(me >= d)(functools.partial(do, d))

    for n in range(NCH):
        w_load(n).wait()
        if n == 0:
            z_own(n)
            y_copy(n, z).start()
            each_other(lambda d: i_copy(d).start())
    load.wait()

    step = 16

    def norm_rows(i, carry):
        at = pl.ds(pl.multiple_of(i * step, step), step)
        total = jnp.zeros((step, CW), jnp.float32)
        for b in range(width // CW):
            v = hidden_ref[at, b * CW : (b + 1) * CW].astype(jnp.float32)
            total = total + v * v
        scale = lax.rsqrt(jnp.sum(total, axis=1, keepdims=True) * (1.0 / width) + 1e-05)
        for b in range(width // depth):
            v = hidden_ref[at, b * depth : (b + 1) * depth].astype(jnp.float32)
            g = gain32[:, b * depth : (b + 1) * depth]
            nsend[PLACE[b % 4], at, (b // 4) * depth : (b // 4 + 1) * depth] = (
                v * scale * g
            ).astype(jnp.bfloat16)
        return carry


    def h_copy(i):
        k, part_at = i % 3, pl.ds((i // 3) * (rows // 2), rows // 2)
        dx, dc = ((1, 0), (1, 1), (0, 1))[k]
        ox = 1 - x if dx else x
        oc = 1 - c if dc else c
        return remote(
            nsend.at[2 * oc + ox, part_at], xg.at[spot, part_at], h_send.at[i], h_recv.at[i],
            z * 8 + y * 4 + ox * 2 + oc,
        )

    for i in range(2):
        lax.fori_loop(i * rows // step // 2, (i + 1) * rows // step // 2, norm_rows, 0)
        for k in range(3):
            h_copy(3 * i + k).start()
    own = pltpu.make_async_copy(nsend.at[spot], xg.at[spot], h_own)
    own.start()

    def forward(n):
        for k in range(1, nz):
            for way in (1, -1):
                pass_on(n, k, way)
            if k == 1 and n + 1 < NCH:
                z_own(n + 1)
        if n + 1 < NCH:
            y_copy(n + 1, z).start()

    def matmul(n):
        for dz in range(nz):
            y_copy(n, dz).wait_recv()
        left = xg[...].reshape(4 * rows, xg.shape[2])
        part[n] = jnp.dot(left, wbuf[n], preferred_element_type=jnp.float32).reshape(
            2, 2, rows, CW
        )

    def c_copy(n):
        return remote(part.at[n, 1 - c], crecv.at[n], c_send.at[n], c_recv.at[n], c_dev)

    def x_copy(n):
        return remote(xsend.at[n], xrecv.at[n], x_send.at[n], x_recv.at[n], x_dev)

    def cross(n):
        c_copy(n).wait_recv()
        xsend[n] = part[n, c, 1 - x] + crecv[n, 1 - x]
        x_copy(n).start()

    def finish(n):
        x_copy(n).wait_recv()
        return part[n, c, x] + crecv[n, x] + xrecv[n]

    def attend(head, query):
        keys = kvbuf[:, :, :HD].reshape((back + 1) * rows, HD)
        values = kvbuf[:, :, HD:].reshape((back + 1) * rows, HD)
        scores = (
            lax.dot_general(
                query, keys, (((1,), (1,)), ((), ())), preferred_element_type=jnp.float32
            )
            * (1.0 / math.sqrt(HD))
            + bias[...]
        )
        weights = jnp.exp(scores - jnp.max(scores, axis=1, keepdims=True))
        total = jnp.sum(weights, axis=1, keepdims=True)
        out = jnp.dot(weights.astype(jnp.bfloat16), values, preferred_element_type=jnp.float32)
        outbuf[:, head * HD : (head + 1) * HD] = (out / total).astype(jnp.bfloat16)

    forward(0)
    forward(1)
    forward(2)
    each_other(lambda d: i_copy(d).wait_recv())
    doc_col = jnp.transpose(jnp.broadcast_to(doc, (rows, rows)))
    count = jnp.zeros((rows, 1), jnp.float32)
    for s in range(back + 1):
        near = ids[lax.rem(me + n_dev - back + s, n_dev), 0:1, :]
        seen = doc_col == jnp.where(me + s >= back, near, -1)
        if s == back:
            seen = seen & (
                lax.broadcasted_iota(jnp.int32, (rows, rows), 1)
                <= lax.broadcasted_iota(jnp.int32, (rows, rows), 0)
            )
        bias[:, s * rows : (s + 1) * rows] = jnp.where(seen, 0.0, -1e30)
        count = count + jnp.sum(jnp.where(seen, 1.0, 0.0), axis=1, keepdims=True)
    angle = (count - 1.0) * freq_ref[...]
    cosine = jnp.cos(angle)
    sine = jnp.sin(angle) * jnp.where(
        lax.broadcasted_iota(jnp.int32, (rows, HD), 1) < HD // 2, -1.0, 1.0
    )

    own.wait()
    for k in range(6):
        h_copy(k).wait_recv()
    matmul(0)
    c_copy(0).start()
    matmul(1)
    c_copy(1).start()
    cross(0)
    cross(1)
    kv = finish(0)
    kvbuf[back, :, :HD] = rotate(kv[:, :HD], cosine, sine).astype(jnp.bfloat16)
    kvbuf[back, :, HD:] = kv[:, HD:].astype(jnp.bfloat16)
    each_later(lambda d: kv_copy(d).start())
    matmul(2)
    c_copy(2).start()
    heads = finish(1)
    cross(2)
    each_earlier(lambda d: kv_copy(d).wait_recv())
    for h in range(2):
        attend(h, rotate(heads[:, h * HD : (h + 1) * HD], cosine, sine).astype(jnp.bfloat16))
    heads = finish(2)
    for h in range(2):
        attend(h + 2, rotate(heads[:, h * HD : (h + 1) * HD], cosine, sine).astype(jnp.bfloat16))

    tgt_mat = jnp.transpose(jnp.broadcast_to(tgt, (rows, rows)))
    earlier = (tgt_mat == tgt) & (
        lax.broadcasted_iota(jnp.int32, (rows, rows), 0)
        < lax.broadcasted_iota(jnp.int32, (rows, rows), 1)
    )
    rank = jnp.sum(jnp.where(earlier, 1.0, 0.0), axis=0, keepdims=True).astype(jnp.int32)
    cap = abuf.shape[1] // 2
    slots = n_dev * 2 * cap
    slot_col = lax.broadcasted_iota(jnp.int32, (slots, rows), 0)
    place = tgt * (2 * cap) + rank
    half = QH * HD // 2
    packed = jnp.dot(
        jnp.where(slot_col == place, 1.0, 0.0).astype(jnp.bfloat16),
        outbuf[:, :half],
        preferred_element_type=jnp.float32,
    ) + jnp.dot(
        jnp.where(slot_col == place + cap, 1.0, 0.0).astype(jnp.bfloat16),
        outbuf[:, half:],
        preferred_element_type=jnp.float32,
    )
    abuf[...] = packed.astype(jnp.bfloat16).reshape(abuf.shape)
    each_other(lambda d: a_copy(d).start())
    rbuf[me] = abuf[me]

    counts = jnp.sum(jnp.where(ids[:, 1, :] == me, 1.0, 0.0), axis=1, keepdims=True)
    lane = lax.broadcasted_iota(jnp.int32, (n_dev, slots), 1)
    source = lax.broadcasted_iota(jnp.int32, (n_dev, slots), 0)
    owner = lane // (2 * cap)
    count_row = jnp.sum(jnp.where(source == owner, counts, 0.0), axis=0, keepdims=True)
    first_row = jnp.sum(jnp.where(source < owner, counts, 0.0), axis=0, keepdims=True)
    inner = lax.broadcasted_iota(jnp.int32, (1, slots), 1) % (2 * cap)
    index = inner % cap
    goal = jnp.where(
        index < count_row.astype(jnp.int32), first_row.astype(jnp.int32) + index, -1
    )
    out_row = lax.broadcasted_iota(jnp.int32, (rows, slots), 0)
    picks = [
        jnp.where(out_row == jnp.where(inner // cap == h, goal, -1), 1.0, 0.0).astype(jnp.bfloat16)
        for h in range(2)
    ]
    each_other(lambda d: a_copy(d).wait_recv())
    arrived = rbuf[...].reshape(slots, half)
    for h in range(2):
        result_ref[:, h * half : (h + 1) * half] = jnp.dot(
            picks[h], arrived, preferred_element_type=jnp.float32
        ).astype(jnp.bfloat16)

    each_other(lambda d: i_copy(d).wait_send())
    each_other(lambda d: a_copy(d).wait_send())
    each_later(lambda d: kv_copy(d).wait_send())
    for k in range(6):
        h_copy(k).wait_send()
    for n in range(NCH):
        for dz in range(nz):
            for way in (1, -1):
                z_left(n, dz, way)
            y_copy(n, dz).wait_send()
        c_copy(n).wait_send()
        x_copy(n).wait_send()


def body(hidden, norm_gain, w_qkv, doc_ids, target):
    n_dev = lax.axis_size("ctx")
    rows, width = hidden.shape
    depth = w_qkv.shape[0]
    cap = 2 * rows // n_dev
    back = -(-(MOST - 1) // rows)
    nz = n_dev // 8
    freqs = 500000.0 ** (-(np.arange(HD // 2, dtype=np.float64) * 2.0) / HD)
    freq_row = jnp.asarray(np.concatenate([freqs, freqs])[None, :], jnp.float32)
    bf16, f32 = jnp.bfloat16, jnp.float32
    dma = pltpu.SemaphoreType.DMA
    return pl.pallas_call(
        functools.partial(kernel, n_dev),
        out_shape=jax.ShapeDtypeStruct((rows, QH * HD), bf16),
        in_specs=[
            pl.BlockSpec(memory_space=pltpu.HBM if i in (0, 2) else pltpu.VMEM) for i in range(6)
        ],
        out_specs=pl.BlockSpec(memory_space=pltpu.VMEM),
        scratch_shapes=[
            pltpu.VMEM((rows, width), bf16),
            pltpu.VMEM((1, width), f32),
            pltpu.VMEM((4, rows, width // 4), bf16),
            pltpu.VMEM((4, rows, width // 4), bf16),
            pltpu.VMEM((NCH, width // 4, CW), bf16),
            pltpu.VMEM((NCH, 2, 2, rows, CW), f32),
            pltpu.VMEM((NCH, 2, rows, CW), f32),
            pltpu.VMEM((NCH, rows, CW), f32),
            pltpu.VMEM((NCH, rows, CW), f32),
            pltpu.VMEM((back + 1, rows, 2 * HD), bf16),
            pltpu.VMEM((n_dev, 8, rows), jnp.int32),
            pltpu.VMEM((rows, (back + 1) * rows), f32),
            pltpu.VMEM((rows, QH * HD), bf16),
            pltpu.VMEM((n_dev, 2 * cap, QH * HD // 2), bf16),
            pltpu.VMEM((n_dev, 2 * cap, QH * HD // 2), bf16),
            dma, dma((NCH,)),
            dma((6,)), dma((6,)), dma,
            dma((NCH, nz, 2)), dma((NCH, nz)), dma((NCH, nz)), dma((NCH, nz)),
            dma((NCH,)), dma((NCH,)), dma((NCH,)), dma((NCH,)),
            dma((back,)), dma((back,)), dma((n_dev,)), dma((n_dev,)), dma((n_dev,)), dma((n_dev,)),
        ],
        compiler_params=pltpu.CompilerParams(
            collective_id=0, has_side_effects=True, vmem_limit_bytes=63 * 1024 * 1024
        ),
        cost_estimate=pl.CostEstimate(
            flops=2 * rows * width * 768, bytes_accessed=4 * 1024 * 1024, transcendentals=0
        ),
    )(
        hidden, norm_gain[None, :], w_qkv, doc_ids[None, :], target[None, :], freq_row
    )


def solution(mesh):
    in_specs = (
        P(("section", "ctx"), None),
        P(),
        P("ctx", None),
        P(("section", "ctx")),
        P(("section", "ctx")),
    )
    out_specs = P(("section", "ctx"), None)
    return jax.shard_map(body, mesh=mesh, in_specs=in_specs, out_specs=out_specs, check_vma=False)
```
